512 devices in a mesh: tm: 64 (over y, z), grp: 8 (over x, core).
Axes of the slice: x: 4, y: 4, z: 16, core: 2. Of those that a mesh axis runs over, the one named last changes fastest.
Arguments:
- records: bfloat16 [2048, 8192], P(('tm', 'grp'))
- band_edges: int32 [4, 2], replicated, may hold values from 2 to 118, as said below
- receiver_block: int32 [64, 9], P('tm'), may hold values from 0 to 63, as said below
- slot_count: int32 [64], P('tm'), may hold values from 5 to 9, as said below
Outputs:
- correlations: float32 [576, 128, 2001], P('tm', 'grp')
The draws below stay inside these ranges and needn't reach their ends.
Inputs may be any that keep to these rules, and one draw needn't show every extreme that they name: Band b passes from band_edges[b, 0] to band_edges[b, 1] in units of 1/256 cycle a sample; the lower edge is below the upper one by 8 or more. `receiver_block`: each receiver block lies within 4 blocks of its source block o (the row index); both distances 4 and - 4 occur in live slots. Slots k < slot_count[o] are live, the others unused; some source block uses all 9 slots.
All inputs are finite; a program needn't handle non-finite values.
Results may differ from the reference program's by a relative error of at most 0.0033.
Values may be sent and summed in bfloat16 or wider, within the bound.
No kernel may reach another device: no remote copies, remote signals or barrier semaphores. Data moves between devices by JAX's collectives and lax.ppermute only.
A program may use at most 64 MiB of HBM per device.

```python
import math
import jax
import jax.numpy as jnp
from jax import lax

BLK = 128
S = 2048
TAPS = 101
NB = 4
LAG = 1000
R = 4
PMAX = 9
CHANNELS = 8192
HALF = 50
LAGS = 2001
N_TM = 64


def draw_records(key, part):
    first_key, second_key, third_key = jax.random.split(key, 3)
    channel_scale = jnp.exp(jax.random.uniform(second_key, (CHANNELS,), minval=0.0, maxval=math.log(10.0)))
    envelope = jnp.exp(jax.random.uniform(third_key, (S // 32, 1), minval=0.0, maxval=math.log(10.0)))
    envelope = jnp.repeat(envelope, 32, axis=0)
    noise = jax.random.normal(first_key, (S, CHANNELS))
    values = 0.1 * noise * channel_scale[None, :] * envelope
    return values.astype(jnp.float32).astype(jnp.bfloat16)


def draw_band_edges(key, part):
    first_key, second_key, third_key = jax.random.split(key, 3)
    lower_band_edge = jax.random.randint(first_key, (NB,), 2, 60)
    band_width = jax.random.randint(second_key, (NB,), 8, 60)
    chosen = jax.random.permutation(third_key, NB)
    lower_band_edge = lower_band_edge.at[chosen[0]].set(2)
    upper_edge = lower_band_edge + band_width
    upper_edge = upper_edge.at[chosen[1]].set(118)
    return jnp.stack([lower_band_edge, upper_edge], axis=1).astype(jnp.int32)


def draw_receiver_block(key, part):
    first_key, second_key, third_key = jax.random.split(key, 3)
    anchor = jnp.arange(N_TM, dtype=jnp.int32)[:, None]
    lowest = jnp.maximum(-R, -anchor)
    highest = jnp.minimum(R, N_TM - 1 - anchor)
    lowest = jnp.broadcast_to(lowest, (N_TM, PMAX))
    highest = jnp.broadcast_to(highest, (N_TM, PMAX))
    distance = jax.random.randint(first_key, (N_TM, PMAX), lowest, highest + 1)
    upper_owner = jax.random.randint(second_key, (), 0, N_TM // 2)
    lower_owner = jax.random.randint(third_key, (), N_TM // 2, N_TM)
    distance = distance.at[upper_owner, 0].set(R)
    distance = distance.at[lower_owner, 0].set(-R)
    return (anchor + distance).astype(jnp.int32)


def draw_slot_count(key, part):
    first_key, second_key = jax.random.split(key, 2)
    counted = jax.random.randint(first_key, (N_TM,), max(1, PMAX - 4), PMAX + 1)
    fullest = jax.random.randint(second_key, (), 0, N_TM)
    return counted.at[fullest].set(PMAX).astype(jnp.int32)


def setup_inputs(seed: int = 0) -> dict:
    keys = jax.random.split(jax.random.key(seed), 5)
    return {
        "records": draw_records(jax.random.fold_in(keys[4], 71), 0),
        "band_edges": draw_band_edges(jax.random.fold_in(keys[4], 71), 0),
        "receiver_block": draw_receiver_block(jax.random.fold_in(keys[4], 71), 0),
        "slot_count": draw_slot_count(jax.random.fold_in(keys[4], 71), 0),
    }


def design_taps(band_edges):
    sample_index = jnp.arange(TAPS).astype(jnp.float32)
    offset = sample_index - HALF
    frequency = band_edges.astype(jnp.float32) / 256.0
    lower_band_edge = frequency[:, 0:1]
    upper_edge = frequency[:, 1:2]
    safe_offset = jnp.where(offset == 0, 1.0, offset)
    ideal_taps = (jnp.sin(2.0 * math.pi * upper_edge * safe_offset) - jnp.sin(2.0 * math.pi * lower_band_edge * safe_offset)) / (math.pi * safe_offset)
    ideal_taps = jnp.where(offset == 0, 2.0 * (upper_edge - lower_band_edge), ideal_taps)
    hamming = 0.54 - 0.46 * jnp.cos(2.0 * math.pi * sample_index / (TAPS - 1))
    return (ideal_taps * hamming).astype(jnp.bfloat16)

def reference(records, band_edges, receiver_block, slot_count):
    filter_taps = design_taps(band_edges).astype(jnp.float32)
    filter_kernel = filter_taps[:, ::-1][:, None, :]
    row_samples = jnp.transpose(records).reshape(N_TM, BLK, S)

    def whiten_block(block_row_list):
        signal = block_row_list.astype(jnp.float32)[:, None, :]
        banded = lax.conv_general_dilated(signal, filter_kernel, (1,), [(HALF, HALF)], dimension_numbers=('NCH', 'OIH', 'NCH'), precision=lax.Precision.HIGHEST)
        band_power = lax.optimization_barrier(jnp.mean(banded * banded, axis=-1, keepdims=True))
        return lax.optimization_barrier(jnp.sum(banded * lax.rsqrt(band_power + 1e-06), axis=1)).astype(jnp.bfloat16)
    whitened = lax.map(whiten_block, row_samples)
    fft_length = 2 * S
    spectra = jnp.fft.rfft(whitened.astype(jnp.float32), n=fft_length, axis=-1)
    lag_scale = 1.0 / (NB * math.sqrt(S))

    def owner_block(anchor):
        source_spectrum = spectra[anchor]
        receiver_spectra = spectra[receiver_block[anchor]]
        circular = jnp.fft.irfft(jnp.conj(source_spectrum)[None] * receiver_spectra, n=fft_length, axis=-1)
        lag_values = jnp.concatenate([circular[..., fft_length - LAG:], circular[..., :LAG + 1]], axis=-1) * lag_scale
        live_slots = jnp.arange(PMAX) < slot_count[anchor]
        return jnp.where(live_slots[:, None, None], lag_values, 0.0)
    result = lax.map(owner_block, jnp.arange(N_TM))
    return result.reshape(N_TM * PMAX, BLK, LAGS).astype(jnp.float32)
```

```python
import math

import jax
import jax.numpy as jnp
from jax import lax
from jax.experimental import pallas as pl
from jax.experimental.pallas import tpu as pltpu
from jax.sharding import PartitionSpec as P

TAPS = 101
NB = 4
LAG = 1000
R = 4
PMAX = 9
HALF = 50
LAGS = 2001
SAMPLES = 2048
SHIFT = 24
VMEM_LIMIT = 48 * 1024 * 1024


def taps_row(band_edges):
    tap = 178 - jnp.arange(384)
    sample_index = tap.astype(jnp.float32)
    offset = sample_index - HALF
    frequency = band_edges.astype(jnp.float32) / 256.0
    lower = frequency[:, 0:1]
    upper = frequency[:, 1:2]
    safe = jnp.where(offset == 0, 1.0, offset)
    ideal = (
        jnp.sin(2.0 * math.pi * upper * safe) - jnp.sin(2.0 * math.pi * lower * safe)
    ) / (math.pi * safe)
    ideal = jnp.where(offset == 0, 2.0 * (upper - lower), ideal)
    hamming = 0.54 - 0.46 * jnp.cos(2.0 * math.pi * sample_index / (TAPS - 1))
    taps = (ideal * hamming).astype(jnp.bfloat16)
    live = (tap >= 0) & (tap < TAPS)
    return jnp.where(live[None, :], taps, jnp.bfloat16(0)).astype(jnp.float32)


def strided(row, rows):
    wide = jnp.broadcast_to(row, (rows, row.shape[1]))
    return pltpu.roll(wide, 0, 1, stride=1, stride_axis=0)


def filter_kernel(taps_ref, out_ref):
    natural = lax.broadcasted_iota(jnp.int32, (128, 128), 0)
    order = lax.broadcasted_iota(jnp.int32, (128, 128), 1)
    time = ((order >> 2) & 3) * 32 + (order >> 4) * 4 + (order & 3)
    pick = (natural == time).astype(jnp.bfloat16)
    lane = lax.broadcasted_iota(jnp.int32, (128, 128), 1)
    row = lax.broadcasted_iota(jnp.int32, (128, 128), 0)
    for band in range(NB):
        before = None
        for part in range(3):
            piece = taps_ref[band : band + 1, part * 128 : (part + 1) * 128]
            rolled = strided(piece, 128)
            last = jnp.zeros_like(rolled) if before is None else before
            block = jnp.where(lane >= row, rolled, last).astype(jnp.bfloat16)
            ordered = jnp.dot(block, pick, preferred_element_type=jnp.float32)
            out_ref[band * 128 : (band + 1) * 128, part * 128 : (part + 1) * 128] = ordered.astype(jnp.bfloat16)
            before = rolled


def shuffle_kernel(x_ref, out_ref):
    group = lax.broadcasted_iota(jnp.int32, (16, 128), 1) >> 4
    for n in range(3):
        for tile in range(2):
            rows = []
            for b in range(8 * tile, 8 * tile + 8):
                parts = [x_ref[4 * b + q, n].astype(jnp.float32) for q in range(4)]
                rows.append(jnp.concatenate(parts, axis=0))
            for g in range(8):
                total = None
                for l in range(8):
                    turn = (16 * (l - g)) % 128
                    moved = rows[l] if turn == 0 else pltpu.roll(rows[l], turn, 1)
                    total = moved if total is None else jnp.where(group == l, moved, total)
                out_ref[g, 16 * n : 16 * n + 16, 128 * tile : 128 * tile + 128] = total.astype(jnp.bfloat16)


def whiten_kernel(filter_ref, x_ref, out_ref):
    lane = lax.broadcasted_iota(jnp.int32, (128, 256), 1)
    for n in range(3):
        here = jnp.concatenate([x_ref[g, 16 * n : 16 * n + 16, :] for g in range(8)], axis=0)
        wide = here.astype(jnp.float32)
        before = jnp.where(lane < 16, 0.0, pltpu.roll(wide, 16, 1)).astype(jnp.bfloat16)
        after = jnp.where(lane >= 240, 0.0, pltpu.roll(wide, 240, 1)).astype(jnp.bfloat16)
        window = jnp.concatenate([before, here, after], axis=0)
        total = None
        for band in range(NB):
            banded = jnp.dot(
                filter_ref[band * 128 : (band + 1) * 128, :], window, preferred_element_type=jnp.float32
            )
            power = jnp.sum(banded * banded, axis=0, keepdims=True)
            power = jnp.broadcast_to(power, (8, 256))
            for turn in (128, 64, 32, 16):
                power = power + pltpu.roll(power, turn, 1)
            scale = lax.rsqrt(power[0:1] * (1.0 / SAMPLES) + 1e-06)
            term = banded * scale
            total = term if total is None else total + term
        turned = jnp.concatenate([total[:, :128].T, total[:, 128:].T], axis=0)
        out_ref[256 * n : 256 * n + 256, :] = turned.astype(jnp.bfloat16)


def correlate_kernel(place_ref, left_ref, own_ref, right_ref, out_ref, rec, src, lhs, toe, res_a, res_b):
    zeros = jnp.zeros((128, 128), jnp.float32)
    for k in range(PMAX + 1):
        rec[pl.ds(k * 512, 128), :] = zeros
        rec[pl.ds(k * 512 + 384, 128), :] = zeros
        if k == PMAX:
            rec[pl.ds(k * 512 + 128, 128), :] = zeros
            rec[pl.ds(k * 512 + 256, 128), :] = zeros
            continue
        place = place_ref[k]
        row = pl.multiple_of(place_ref[16 + k], 256)

        @pl.when(place == -1)
        def _():
            rec[pl.ds(k * 512 + 128, 128), :] = zeros
            rec[pl.ds(k * 512 + 256, 128), :] = zeros

        for side, ref in enumerate((left_ref, own_ref, right_ref)):

            @pl.when(place == side)
            def _():
                rec[pl.ds(k * 512 + 128, 256), :] = ref[pl.ds(row, 256), :].astype(jnp.float32)

    src[...] = own_ref[256:512, :].astype(jnp.float32)
    zero_tile = jnp.zeros((128, 128), jnp.bfloat16)
    toe[128:256, 0:128] = zero_tile
    toe[0:128, 17 * 128 : 18 * 128] = zero_tile
    lane = lax.broadcasted_iota(jnp.int32, (128, 128), 1)
    line = lax.broadcasted_iota(jnp.int32, (128, 128), 0)
    lag_scale = 1.0 / (NB * math.sqrt(SAMPLES))

    def channel(c, carry):
        before = jnp.zeros((128, 128), jnp.float32)
        for b in range(17):
            if b < 16:
                rolled = strided(src[pl.ds(b * 16 + c, 1), :], 128)
            else:
                rolled = jnp.zeros((128, 128), jnp.float32)
            tile = jnp.where(lane >= line, rolled, before).astype(jnp.bfloat16)
            toe[0:128, 128 * b : 128 * b + 128] = tile
            toe[128:256, 128 * b + 128 : 128 * b + 256] = tile
            before = rolled
        for b in range(18):
            for pair in range(5):
                parts = [
                    rec[pl.ds((k * 32 + b) * 16 + c, 8, stride=32), :] for k in (2 * pair, 2 * pair + 1)
                ]
                lhs[16 * pair : 16 * pair + 16, 128 * b : 128 * b + 128] = jnp.concatenate(parts, axis=0).astype(
                    jnp.bfloat16
                )
        found = lax.dot_general(
            lhs[...], toe[...], (((1,), (1,)), ((), ())), preferred_element_type=jnp.float32
        )
        for k in range(PMAX):
            piece = found[8 * k : 8 * k + 8, :] * lag_scale
            res_a[pl.ds(k * 128 + c, 8, stride=16), :] = piece[:, :128]
            res_b[pl.ds(k * 128 + c, 8, stride=16), :] = piece[:, 128:]
        return carry

    lax.fori_loop(0, 16, channel, 0)
    for k in range(PMAX):
        parts = []
        for m in range(8):
            parts.append(res_a[k * 128 + 16 * m : k * 128 + 16 * m + 16, :])
            parts.append(res_b[k * 128 + 16 * m : k * 128 + 16 * m + 16, :])
        out_ref[k] = jnp.concatenate(parts, axis=1)[:, SHIFT : SHIFT + LAGS]


def call(kernel, out, args, scalars=0, scratch=(), flops=0):
    vmem = pl.BlockSpec(memory_space=pltpu.VMEM)
    smem = pl.BlockSpec(memory_space=pltpu.SMEM)
    size = sum(math.prod(a.shape) * a.dtype.itemsize for a in args) + math.prod(out.shape) * out.dtype.itemsize
    return pl.pallas_call(
        kernel,
        out_shape=out,
        in_specs=[smem] * scalars + [vmem] * (len(args) - scalars),
        out_specs=vmem,
        scratch_shapes=list(scratch),
        compiler_params=pltpu.CompilerParams(vmem_limit_bytes=VMEM_LIMIT),
        cost_estimate=pl.CostEstimate(flops=flops, bytes_accessed=size, transcendentals=0),
    )(*args)


def on_device(records, band_edges, receiver_block, slot_count):
    bf16 = jnp.bfloat16
    mine = records.reshape(4, 64, 128).transpose(1, 0, 2)
    sent = jnp.stack([jnp.roll(mine, 3, 0), mine, jnp.roll(mine, -3, 0)], axis=1)
    got = lax.all_to_all(sent, "tm", 0, 0, tiled=True)
    filters = call(
        filter_kernel, jax.ShapeDtypeStruct((512, 384), bf16), (taps_row(band_edges),), flops=2 * 512 * 384 * 128
    )
    shuffled = call(shuffle_kernel, jax.ShapeDtypeStruct((8, 48, 256), bf16), (got,))
    rows = lax.all_to_all(shuffled, "grp", 0, 0, tiled=True)
    own = call(
        whiten_kernel, jax.ShapeDtypeStruct((768, 128), bf16), (filters, rows), flops=2 * 3 * 512 * 384 * 256
    )
    size = lax.axis_size("tm")
    left = lax.ppermute(own, "tm", [(i, (i + 1) % size) for i in range(size)])
    right = lax.ppermute(own, "tm", [(i, (i - 1) % size) for i in range(size)])
    position = jnp.clip(receiver_block[0] - lax.axis_index("tm") + R, 0, 2 * R)
    live = jnp.arange(PMAX) < slot_count[0]
    places = jnp.concatenate(
        [
            jnp.where(live, position % 3, -1),
            jnp.zeros((16 - PMAX,), jnp.int32),
            256 * (position // 3),
            jnp.zeros((16 - PMAX,), jnp.int32),
        ]
    ).astype(jnp.int32)
    return call(
        correlate_kernel,
        jax.ShapeDtypeStruct((PMAX, 16, LAGS), jnp.float32),
        (places, left, own, right),
        scalars=1,
        scratch=[
            pltpu.VMEM(((PMAX + 1) * 512, 128), jnp.float32),
            pltpu.VMEM((256, 128), jnp.float32),
            pltpu.VMEM((80, 2304), bf16),
            pltpu.VMEM((256, 2304), bf16),
            pltpu.VMEM((PMAX * 128, 128), jnp.float32),
            pltpu.VMEM((PMAX * 128, 128), jnp.float32),
        ],
        flops=2 * 16 * 80 * 2304 * 256,
    )


def solution(mesh):
    return jax.shard_map(
        on_device,
        mesh=mesh,
        in_specs=(P(("tm", "grp"), None), P(), P("tm", None), P("tm")),
        out_specs=P("tm", "grp", None),
        check_vma=False,
    )
```

```python
import math

import jax
import jax.numpy as jnp
from jax import lax
from jax.experimental import pallas as pl
from jax.experimental.pallas import tpu as pltpu
from jax.sharding import PartitionSpec as P

TAPS = 101
NB = 4
LAG = 1000
R = 4
PMAX = 9
HALF = 50
LAGS = 2001
SAMPLES = 2048
SHIFT = 24
VMEM_LIMIT = 32 * 1024 * 1024


def taps_row(band_edges):
    tap = 178 - jnp.arange(384)
    sample_index = tap.astype(jnp.float32)
    offset = sample_index - HALF
    frequency = band_edges.astype(jnp.float32) / 256.0
    lower = frequency[:, 0:1]
    upper = frequency[:, 1:2]
    safe = jnp.where(offset == 0, 1.0, offset)
    ideal = (
        jnp.sin(2.0 * math.pi * upper * safe) - jnp.sin(2.0 * math.pi * lower * safe)
    ) / (math.pi * safe)
    ideal = jnp.where(offset == 0, 2.0 * (upper - lower), ideal)
    hamming = 0.54 - 0.46 * jnp.cos(2.0 * math.pi * sample_index / (TAPS - 1))
    taps = (ideal * hamming).astype(jnp.bfloat16)
    live = (tap >= 0) & (tap < TAPS)
    return jnp.where(live[None, :], taps, jnp.bfloat16(0)).astype(jnp.float32)


def strided(row, rows):
    wide = jnp.broadcast_to(row, (rows, row.shape[1]))
    return pltpu.roll(wide, 0, 1, stride=1, stride_axis=0)


def filter_kernel(taps_ref, out_ref):
    natural = lax.broadcasted_iota(jnp.int32, (128, 128), 0)
    order = lax.broadcasted_iota(jnp.int32, (128, 128), 1)
    time = ((order >> 2) & 3) * 32 + (order >> 4) * 4 + (order & 3)
    pick = (natural == time).astype(jnp.bfloat16)
    lane = lax.broadcasted_iota(jnp.int32, (128, 128), 1)
    row = lax.broadcasted_iota(jnp.int32, (128, 128), 0)
    for band in range(NB):
        before = None
        for part in range(3):
            piece = taps_ref[band : band + 1, part * 128 : (part + 1) * 128]
            rolled = strided(piece, 128)
            last = jnp.zeros_like(rolled) if before is None else before
            block = jnp.where(lane >= row, rolled, last).astype(jnp.bfloat16)
            ordered = jnp.dot(block, pick, preferred_element_type=jnp.float32)
            out_ref[band * 128 : (band + 1) * 128, part * 128 : (part + 1) * 128] = ordered.astype(jnp.bfloat16)
            before = rolled


def shuffle_kernel(x_ref, out_ref):
    group = lax.broadcasted_iota(jnp.int32, (16, 128), 1) >> 4
    for n in range(3):
        for tile in range(2):
            rows = []
            for b in range(8 * tile, 8 * tile + 8):
                parts = [x_ref[4 * b + q, n].astype(jnp.float32) for q in range(4)]
                rows.append(jnp.concatenate(parts, axis=0))
            for g in range(8):
                total = None
                for l in range(8):
                    turn = (16 * (l - g)) % 128
                    moved = rows[l] if turn == 0 else pltpu.roll(rows[l], turn, 1)
                    total = moved if total is None else jnp.where(group == l, moved, total)
                out_ref[g, 16 * n : 16 * n + 16, 128 * tile : 128 * tile + 128] = total.astype(jnp.bfloat16)


def whiten_kernel(filter_ref, x_ref, out_ref):
    lane = lax.broadcasted_iota(jnp.int32, (128, 256), 1)
    for n in range(3):
        here = jnp.concatenate([x_ref[g, 16 * n : 16 * n + 16, :] for g in range(8)], axis=0)
        wide = here.astype(jnp.float32)
        before = jnp.where(lane < 16, 0.0, pltpu.roll(wide, 16, 1)).astype(jnp.bfloat16)
        after = jnp.where(lane >= 240, 0.0, pltpu.roll(wide, 240, 1)).astype(jnp.bfloat16)
        window = jnp.concatenate([before, here, after], axis=0)
        total = None
        for band in range(NB):
            banded = jnp.dot(
                filter_ref[band * 128 : (band + 1) * 128, :], window, preferred_element_type=jnp.float32
            )
            power = jnp.sum(banded * banded, axis=0, keepdims=True)
            power = jnp.broadcast_to(power, (8, 256))
            for turn in (128, 64, 32, 16):
                power = power + pltpu.roll(power, turn, 1)
            scale = lax.rsqrt(power[0:1] * (1.0 / SAMPLES) + 1e-06)
            term = banded * scale
            total = term if total is None else total + term
        turned = jnp.concatenate([total[:, :128].T, total[:, 128:].T], axis=0)
        out_ref[256 * n : 256 * n + 256, :] = turned.astype(jnp.bfloat16)


def spread_kernel(x_ref, out_ref):
    for o in range(64):
        block = x_ref[:, 128 * o : 128 * o + 128]
        out_ref[(o + 3) % 64, 0] = block
        out_ref[o, 1] = block
        out_ref[(o - 3) % 64, 2] = block


def toeplitz_kernel(own_ref, out_ref, src):
    line = lax.broadcasted_iota(jnp.int32, (128, 128), 0)
    lane = lax.broadcasted_iota(jnp.int32, (128, 128), 1)
    turn = (line + lane == 127).astype(jnp.bfloat16)
    src[...] = jnp.dot(own_ref[256:512, :], turn, preferred_element_type=jnp.float32)
    zero_tile = jnp.zeros((128, 128), jnp.bfloat16)

    def channel(c, carry):
        before = jnp.zeros((128, 128), jnp.float32)
        out_ref[c, 0:128, :] = zero_tile
        for e in range(17):
            if e < 16:
                wide = jnp.broadcast_to(src[pl.ds(e * 16 + c, 1), :], (128, 128))
                rolled = pltpu.roll(wide, 1, 1, stride=1, stride_axis=0)
            else:
                rolled = jnp.zeros((128, 128), jnp.float32)
            tile = jnp.where(lane <= line, rolled, before).astype(jnp.bfloat16)
            out_ref[c, 128 * e + 128 : 128 * e + 256, :] = tile
            before = rolled
        out_ref[c, 18 * 128 : 19 * 128, :] = zero_tile
        return carry

    lax.fori_loop(0, 16, channel, 0)


def correlate_kernel(place_ref, toe_ref, left_ref, own_ref, right_ref, out_ref, rec, lhs_0, lhs_1, res_a, res_b):
    zeros = jnp.zeros((128, 128), jnp.float32)
    for k in range(PMAX + 1):
        rec[pl.ds(k * 512, 128), :] = zeros
        rec[pl.ds(k * 512 + 384, 128), :] = zeros
        if k == PMAX:
            rec[pl.ds(k * 512 + 128, 128), :] = zeros
            rec[pl.ds(k * 512 + 256, 128), :] = zeros
            continue
        place = place_ref[k]
        row = pl.multiple_of(place_ref[16 + k], 256)

        @pl.when(place == -1)
        def _():
            rec[pl.ds(k * 512 + 128, 128), :] = zeros
            rec[pl.ds(k * 512 + 256, 128), :] = zeros

        for side, ref in enumerate((left_ref, own_ref, right_ref)):

            @pl.when(place == side)
            def _():
                rec[pl.ds(k * 512 + 128, 256), :] = ref[pl.ds(row, 256), :].astype(jnp.float32)

    lag_scale = 1.0 / (NB * math.sqrt(SAMPLES))

    def fill(lhs, c):
        for b in range(18):
            for pair in range(5):
                parts = [
                    rec[pl.ds((k * 32 + b) * 16 + c, 8, stride=32), :] for k in (2 * pair, 2 * pair + 1)
                ]
                lhs[16 * pair : 16 * pair + 16, 128 * b : 128 * b + 128] = jnp.concatenate(parts, axis=0).astype(
                    jnp.bfloat16
                )

    def work(lhs, c):
        matrix = jnp.concatenate([toe_ref[c, 128:2432, :], toe_ref[c, 0:2304, :]], axis=1)
        found = jnp.dot(lhs[...], matrix, preferred_element_type=jnp.float32)
        for k in range(PMAX):
            piece = found[8 * k : 8 * k + 8, :] * lag_scale
            res_a[pl.ds(k * 128 + c, 8, stride=16), :] = piece[:, :128]
            res_b[pl.ds(k * 128 + c, 8, stride=16), :] = piece[:, 128:]

    def two(i, carry):
        fill(lhs_0, 2 * i)
        fill(lhs_1, 2 * i + 1)
        work(lhs_0, 2 * i)
        work(lhs_1, 2 * i + 1)
        return carry

    lax.fori_loop(0, 8, two, 0)
    for k in range(PMAX):
        parts = []
        for m in range(8):
            parts.append(res_a[k * 128 + 16 * m : k * 128 + 16 * m + 16, :])
            parts.append(res_b[k * 128 + 16 * m : k * 128 + 16 * m + 16, :])
        out_ref[k] = jnp.concatenate(parts, axis=1)[:, SHIFT : SHIFT + LAGS]


def call(kernel, out, args, scalars=0, scratch=(), flops=0):
    vmem = pl.BlockSpec(memory_space=pltpu.VMEM)
    smem = pl.BlockSpec(memory_space=pltpu.SMEM)
    size = sum(math.prod(a.shape) * a.dtype.itemsize for a in args) + math.prod(out.shape) * out.dtype.itemsize
    return pl.pallas_call(
        kernel,
        out_shape=out,
        in_specs=[smem] * scalars + [vmem] * (len(args) - scalars),
        out_specs=vmem,
        scratch_shapes=list(scratch),
        compiler_params=pltpu.CompilerParams(vmem_limit_bytes=VMEM_LIMIT),
        cost_estimate=pl.CostEstimate(flops=flops, bytes_accessed=size, transcendentals=0),
    )(*args)


def on_device(records, band_edges, receiver_block, slot_count):
    bf16 = jnp.bfloat16
    sent = call(spread_kernel, jax.ShapeDtypeStruct((64, 3, 4, 128), bf16), (records,))
    got = lax.all_to_all(sent, "tm", 0, 0, tiled=True)
    filters = call(
        filter_kernel, jax.ShapeDtypeStruct((512, 384), bf16), (taps_row(band_edges),), flops=2 * 512 * 384 * 128
    )
    shuffled = call(shuffle_kernel, jax.ShapeDtypeStruct((8, 48, 256), bf16), (got,))
    rows = lax.all_to_all(shuffled, "grp", 0, 0, tiled=True)
    own = call(
        whiten_kernel, jax.ShapeDtypeStruct((768, 128), bf16), (filters, rows), flops=2 * 3 * 512 * 384 * 256
    )
    size = lax.axis_size("tm")
    left = lax.ppermute(own, "tm", [(i, (i + 1) % size) for i in range(size)])
    right = lax.ppermute(own, "tm", [(i, (i - 1) % size) for i in range(size)])
    toe = call(
        toeplitz_kernel,
        jax.ShapeDtypeStruct((16, 2432, 128), bf16),
        (own,),
        scratch=[pltpu.VMEM((256, 128), jnp.float32)],
        flops=2 * 16 * 2432 * 128 * 256,
    )
    position = jnp.clip(receiver_block[0] - lax.axis_index("tm") + R, 0, 2 * R)
    live = jnp.arange(PMAX) < slot_count[0]
    places = jnp.concatenate(
        [
            jnp.where(live, position % 3, -1),
            jnp.zeros((16 - PMAX,), jnp.int32),
            256 * (position // 3),
            jnp.zeros((16 - PMAX,), jnp.int32),
        ]
    ).astype(jnp.int32)
    return call(
        correlate_kernel,
        jax.ShapeDtypeStruct((PMAX, 16, LAGS), jnp.float32),
        (places, toe, left, own, right),
        scalars=1,
        scratch=[
            pltpu.VMEM(((PMAX + 1) * 512, 128), jnp.float32),
            pltpu.VMEM((80, 2304), bf16),
            pltpu.VMEM((80, 2304), bf16),
            pltpu.VMEM((PMAX * 128, 128), jnp.float32),
            pltpu.VMEM((PMAX * 128, 128), jnp.float32),
        ],
        flops=2 * 16 * 80 * 2304 * 256,
    )


def solution(mesh):
    return jax.shard_map(
        on_device,
        mesh=mesh,
        in_specs=(P(("tm", "grp"), None), P(), P("tm", None), P("tm")),
        out_specs=P("tm", "grp", None),
        check_vma=False,
    )
```

```python
import math

import jax
import jax.numpy as jnp
from jax import lax
from jax.experimental import pallas as pl
from jax.experimental.pallas import tpu as pltpu
from jax.sharding import PartitionSpec as P

TAPS = 101
NB = 4
LAG = 1000
R = 4
PMAX = 9
HALF = 50
LAGS = 2001
SAMPLES = 2048
SHIFT = 24
VMEM_LIMIT = 32 * 1024 * 1024


def taps_row(band_edges):
    tap = 178 - jnp.arange(384)
    sample_index = tap.astype(jnp.float32)
    offset = sample_index - HALF
    frequency = band_edges.astype(jnp.float32) / 256.0
    lower = frequency[:, 0:1]
    upper = frequency[:, 1:2]
    safe = jnp.where(offset == 0, 1.0, offset)
    ideal = (
        jnp.sin(2.0 * math.pi * upper * safe) - jnp.sin(2.0 * math.pi * lower * safe)
    ) / (math.pi * safe)
    ideal = jnp.where(offset == 0, 2.0 * (upper - lower), ideal)
    hamming = 0.54 - 0.46 * jnp.cos(2.0 * math.pi * sample_index / (TAPS - 1))
    taps = (ideal * hamming).astype(jnp.bfloat16)
    live = (tap >= 0) & (tap < TAPS)
    return jnp.where(live[None, :], taps, jnp.bfloat16(0)).astype(jnp.float32)


def strided(row, rows):
    wide = jnp.broadcast_to(row, (rows, row.shape[1]))
    return pltpu.roll(wide, 0, 1, stride=1, stride_axis=0)


def filter_kernel(taps_ref, out_ref):
    natural = lax.broadcasted_iota(jnp.int32, (128, 128), 0)
    order = lax.broadcasted_iota(jnp.int32, (128, 128), 1)
    time = ((order >> 2) & 3) * 32 + (order >> 4) * 4 + (order & 3)
    pick = (natural == time).astype(jnp.bfloat16)
    lane = lax.broadcasted_iota(jnp.int32, (128, 128), 1)
    row = lax.broadcasted_iota(jnp.int32, (128, 128), 0)
    for band in range(NB):
        before = None
        for part in range(3):
            piece = taps_ref[band : band + 1, part * 128 : (part + 1) * 128]
            rolled = strided(piece, 128)
            last = jnp.zeros_like(rolled) if before is None else before
            block = jnp.where(lane >= row, rolled, last).astype(jnp.bfloat16)
            ordered = jnp.dot(block, pick, preferred_element_type=jnp.float32)
            out_ref[band * 128 : (band + 1) * 128, part * 128 : (part + 1) * 128] = ordered.astype(jnp.bfloat16)
            before = rolled


def shuffle_kernel(x_ref, out_ref):
    group = lax.broadcasted_iota(jnp.int32, (16, 128), 1) >> 4
    for n in range(3):
        for tile in range(2):
            rows = []
            for b in range(8 * tile, 8 * tile + 8):
                parts = [x_ref[4 * b + q, n].astype(jnp.float32) for q in range(4)]
                rows.append(jnp.concatenate(parts, axis=0))
            for g in range(8):
                total = None
                for l in range(8):
                    turn = (16 * (l - g)) % 128
                    moved = rows[l] if turn == 0 else pltpu.roll(rows[l], turn, 1)
                    total = moved if total is None else jnp.where(group == l, moved, total)
                out_ref[g, 16 * n : 16 * n + 16, 128 * tile : 128 * tile + 128] = total.astype(jnp.bfloat16)


def whiten_kernel(filter_ref, x_ref, out_ref):
    lane = lax.broadcasted_iota(jnp.int32, (128, 256), 1)
    row = lax.broadcasted_iota(jnp.int32, (256, 256), 0)
    column = lax.broadcasted_iota(jnp.int32, (256, 256), 1)
    wanted = (2 * (row & 7) + ((row >> 3) & 1)) * 16 + (row >> 4)
    pick = (column == wanted).astype(jnp.bfloat16)
    for n in range(3):
        here = jnp.concatenate([x_ref[g, 16 * n : 16 * n + 16, :] for g in range(8)], axis=0)
        wide = here.astype(jnp.float32)
        before = jnp.where(lane < 16, 0.0, pltpu.roll(wide, 16, 1)).astype(jnp.bfloat16)
        after = jnp.where(lane >= 240, 0.0, pltpu.roll(wide, 240, 1)).astype(jnp.bfloat16)
        window = jnp.concatenate([before, here, after], axis=0)
        total = None
        for band in range(NB):
            banded = jnp.dot(
                filter_ref[band * 128 : (band + 1) * 128, :], window, preferred_element_type=jnp.float32
            )
            power = jnp.sum(banded * banded, axis=0, keepdims=True)
            power = jnp.broadcast_to(power, (8, 256))
            for turn in (128, 64, 32, 16):
                power = power + pltpu.roll(power, turn, 1)
            scale = lax.rsqrt(power[0:1] * (1.0 / SAMPLES) + 1e-06)
            term = banded * scale
            total = term if total is None else total + term
        turned = lax.dot_general(
            pick, total.astype(jnp.bfloat16), (((1,), (1,)), ((), ())), preferred_element_type=jnp.float32
        )
        out_ref[256 * n : 256 * n + 256, :] = turned.astype(jnp.bfloat16)


def spread_kernel(x_ref, out_ref):
    for o in range(64):
        block = x_ref[:, 128 * o : 128 * o + 128]
        out_ref[(o + 3) % 64, 0] = block
        out_ref[o, 1] = block
        out_ref[(o - 3) % 64, 2] = block


def toeplitz_kernel(own_ref, out_ref, src):
    line = lax.broadcasted_iota(jnp.int32, (128, 128), 0)
    lane = lax.broadcasted_iota(jnp.int32, (128, 128), 1)
    turn = (line + lane == 127).astype(jnp.bfloat16)
    src[...] = jnp.dot(own_ref[256:512, :], turn, preferred_element_type=jnp.float32)
    zero_tile = jnp.zeros((128, 128), jnp.bfloat16)

    def channel(c, carry):
        before = jnp.zeros((128, 128), jnp.float32)
        out_ref[c, 0:128, :] = zero_tile
        for e in range(17):
            if e < 16:
                wide = jnp.broadcast_to(src[pl.ds(c * 16 + (e % 2) * 8 + e // 2, 1), :], (128, 128))
                rolled = pltpu.roll(wide, 1, 1, stride=1, stride_axis=0)
            else:
                rolled = jnp.zeros((128, 128), jnp.float32)
            tile = jnp.where(lane <= line, rolled, before).astype(jnp.bfloat16)
            out_ref[c, 128 * e + 128 : 128 * e + 256, :] = tile
            before = rolled
        out_ref[c, 18 * 128 : 19 * 128, :] = zero_tile
        return carry

    lax.fori_loop(0, 16, channel, 0)


def correlate_kernel(place_ref, toe_ref, left_ref, own_ref, right_ref, out_ref, rec, lhs_0, lhs_1, res_a, res_b):
    zeros = jnp.zeros((8, 128), jnp.float32)
    for i in range(PMAX * 32 + 1):
        rec[16 * i : 16 * i + 8, :] = zeros
    for k in range(PMAX):
        place = place_ref[k]
        row = pl.multiple_of(place_ref[16 + k], 256)

        @pl.when(place == -1)
        def _():
            for i in range(32):
                rec[(k * 32 + i) * 16 + 8 : (k * 32 + i) * 16 + 16, :] = zeros

        for side, ref in enumerate((left_ref, own_ref, right_ref)):

            @pl.when(place == side)
            def _():
                rows = ref[pl.ds(row, 256), :].astype(jnp.float32)
                for i in range(32):
                    rec[(k * 32 + i) * 16 + 8 : (k * 32 + i) * 16 + 16, :] = rows[8 * i : 8 * i + 8, :]

    lag_scale = 1.0 / (NB * math.sqrt(SAMPLES))

    def fill(lhs, c):
        first = pl.multiple_of(c * 32, 32)
        for b in range(18):
            parts = []
            for k in range(PMAX):
                parts.append(rec[pl.ds(first + (k * 512 + (b % 2) * 16 + 4 + b // 2), 8), :])
            parts.append(zeros)
            for pair in range(5):
                both = jnp.concatenate(parts[2 * pair : 2 * pair + 2], axis=0).astype(jnp.bfloat16)
                lhs[16 * pair : 16 * pair + 16, 128 * b : 128 * b + 128] = both

    def work(lhs, c):
        matrix = jnp.concatenate([toe_ref[c, 128:2432, :], toe_ref[c, 0:2304, :]], axis=1)
        found = jnp.dot(lhs[...], matrix, preferred_element_type=jnp.float32)
        for k in range(PMAX):
            piece = found[8 * k : 8 * k + 8, :] * lag_scale
            res_a[pl.ds(k * 128 + c, 8, stride=16), :] = piece[:, :128]
            res_b[pl.ds(k * 128 + c, 8, stride=16), :] = piece[:, 128:]

    def two(i, carry):
        fill(lhs_0, 2 * i)
        fill(lhs_1, 2 * i + 1)
        work(lhs_0, 2 * i)
        work(lhs_1, 2 * i + 1)
        return carry

    lax.fori_loop(0, 8, two, 0)
    for k in range(PMAX):
        parts = []
        for m in range(8):
            parts.append(res_a[k * 128 + 16 * m : k * 128 + 16 * m + 16, :])
            parts.append(res_b[k * 128 + 16 * m : k * 128 + 16 * m + 16, :])
        out_ref[k] = jnp.concatenate(parts, axis=1)[:, SHIFT : SHIFT + LAGS]


def call(kernel, out, args, scalars=0, scratch=(), flops=0):
    vmem = pl.BlockSpec(memory_space=pltpu.VMEM)
    smem = pl.BlockSpec(memory_space=pltpu.SMEM)
    size = sum(math.prod(a.shape) * a.dtype.itemsize for a in args) + math.prod(out.shape) * out.dtype.itemsize
    return pl.pallas_call(
        kernel,
        out_shape=out,
        in_specs=[smem] * scalars + [vmem] * (len(args) - scalars),
        out_specs=vmem,
        scratch_shapes=list(scratch),
        compiler_params=pltpu.CompilerParams(vmem_limit_bytes=VMEM_LIMIT),
        cost_estimate=pl.CostEstimate(flops=flops, bytes_accessed=size, transcendentals=0),
    )(*args)


def on_device(records, band_edges, receiver_block, slot_count):
    bf16 = jnp.bfloat16
    sent = call(spread_kernel, jax.ShapeDtypeStruct((64, 3, 4, 128), bf16), (records,))
    got = lax.all_to_all(sent, "tm", 0, 0, tiled=True)
    filters = call(
        filter_kernel, jax.ShapeDtypeStruct((512, 384), bf16), (taps_row(band_edges),), flops=2 * 512 * 384 * 128
    )
    shuffled = call(shuffle_kernel, jax.ShapeDtypeStruct((8, 48, 256), bf16), (got,))
    rows = lax.all_to_all(shuffled, "grp", 0, 0, tiled=True)
    own = call(
        whiten_kernel, jax.ShapeDtypeStruct((768, 128), bf16), (filters, rows), flops=2 * 3 * 512 * 384 * 256
    )
    size = lax.axis_size("tm")
    left = lax.ppermute(own, "tm", [(i, (i + 1) % size) for i in range(size)])
    right = lax.ppermute(own, "tm", [(i, (i - 1) % size) for i in range(size)])
    toe = call(
        toeplitz_kernel,
        jax.ShapeDtypeStruct((16, 2432, 128), bf16),
        (own,),
        scratch=[pltpu.VMEM((256, 128), jnp.float32)],
        flops=2 * 16 * 2432 * 128 * 256,
    )
    position = jnp.clip(receiver_block[0] - lax.axis_index("tm") + R, 0, 2 * R)
    live = jnp.arange(PMAX) < slot_count[0]
    places = jnp.concatenate(
        [
            jnp.where(live, position % 3, -1),
            jnp.zeros((16 - PMAX,), jnp.int32),
            256 * (position // 3),
            jnp.zeros((16 - PMAX,), jnp.int32),
        ]
    ).astype(jnp.int32)
    return call(
        correlate_kernel,
        jax.ShapeDtypeStruct((PMAX, 16, LAGS), jnp.float32),
        (places, toe, left, own, right),
        scalars=1,
        scratch=[
            pltpu.VMEM((PMAX * 512 + 8, 128), jnp.float32),
            pltpu.VMEM((80, 2304), bf16),
            pltpu.VMEM((80, 2304), bf16),
            pltpu.VMEM((PMAX * 128, 128), jnp.float32),
            pltpu.VMEM((PMAX * 128, 128), jnp.float32),
        ],
        flops=2 * 16 * 80 * 2304 * 256,
    )


def solution(mesh):
    return jax.shard_map(
        on_device,
        mesh=mesh,
        in_specs=(P(("tm", "grp"), None), P(), P("tm", None), P("tm")),
        out_specs=P("tm", "grp", None),
        check_vma=False,
    )
```

```python
import math

import jax
import jax.numpy as jnp
from jax import lax
from jax.experimental import pallas as pl
from jax.experimental.pallas import tpu as pltpu
from jax.sharding import PartitionSpec as P

TAPS = 101
NB = 4
LAG = 1000
R = 4
PMAX = 9
HALF = 50
LAGS = 2001
SAMPLES = 2048
SHIFT = 24
VMEM_LIMIT = 32 * 1024 * 1024


def taps_row(band_edges):
    tap = 178 - jnp.arange(384)
    sample_index = tap.astype(jnp.float32)
    offset = sample_index - HALF
    frequency = band_edges.astype(jnp.float32) / 256.0
    lower = frequency[:, 0:1]
    upper = frequency[:, 1:2]
    safe = jnp.where(offset == 0, 1.0, offset)
    ideal = (
        jnp.sin(2.0 * math.pi * upper * safe) - jnp.sin(2.0 * math.pi * lower * safe)
    ) / (math.pi * safe)
    ideal = jnp.where(offset == 0, 2.0 * (upper - lower), ideal)
    hamming = 0.54 - 0.46 * jnp.cos(2.0 * math.pi * sample_index / (TAPS - 1))
    taps = (ideal * hamming).astype(jnp.bfloat16)
    live = (tap >= 0) & (tap < TAPS)
    return jnp.where(live[None, :], taps, jnp.bfloat16(0)).astype(jnp.float32)


def strided(row, rows):
    wide = jnp.broadcast_to(row, (rows, row.shape[1]))
    return pltpu.roll(wide, 0, 1, stride=1, stride_axis=0)


def filter_kernel(taps_ref, out_ref):
    natural = lax.broadcasted_iota(jnp.int32, (128, 128), 0)
    order = lax.broadcasted_iota(jnp.int32, (128, 128), 1)
    time = ((order >> 2) & 3) * 32 + (order >> 4) * 4 + (order & 3)
    pick = (natural == time).astype(jnp.bfloat16)
    lane = lax.broadcasted_iota(jnp.int32, (128, 128), 1)
    row = lax.broadcasted_iota(jnp.int32, (128, 128), 0)
    for band in range(NB):
        before = None
        for part in range(3):
            piece = taps_ref[band : band + 1, part * 128 : (part + 1) * 128]
            rolled = strided(piece, 128)
            last = jnp.zeros_like(rolled) if before is None else before
            block = jnp.where(lane >= row, rolled, last).astype(jnp.bfloat16)
            ordered = jnp.dot(block, pick, preferred_element_type=jnp.float32)
            out_ref[band * 128 : (band + 1) * 128, part * 128 : (part + 1) * 128] = ordered.astype(jnp.bfloat16)
            before = rolled


def shuffle_kernel(x_ref, out_ref):
    group = lax.broadcasted_iota(jnp.int32, (16, 128), 1) >> 4
    for n in range(3):
        for tile in range(2):
            rows = []
            for b in range(8 * tile, 8 * tile + 8):
                parts = [x_ref[4 * b + q, n].astype(jnp.float32) for q in range(4)]
                rows.append(jnp.concatenate(parts, axis=0))
            for g in range(8):
                total = None
                for l in range(8):
                    turn = (16 * (l - g)) % 128
                    moved = rows[l] if turn == 0 else pltpu.roll(rows[l], turn, 1)
                    total = moved if total is None else jnp.where(group == l, moved, total)
                out_ref[g, 16 * n : 16 * n + 16, 128 * tile : 128 * tile + 128] = total.astype(jnp.bfloat16)


def whiten_kernel(filter_ref, x_ref, out_ref):
    lane = lax.broadcasted_iota(jnp.int32, (128, 256), 1)
    for n in range(3):
        here = jnp.concatenate([x_ref[g, 16 * n : 16 * n + 16, :] for g in range(8)], axis=0)
        wide = here.astype(jnp.float32)
        before = jnp.where(lane < 16, 0.0, pltpu.roll(wide, 16, 1)).astype(jnp.bfloat16)
        after = jnp.where(lane >= 240, 0.0, pltpu.roll(wide, 240, 1)).astype(jnp.bfloat16)
        window = jnp.concatenate([before, here, after], axis=0)
        total = None
        for band in range(NB):
            banded = jnp.dot(
                filter_ref[band * 128 : (band + 1) * 128, :], window, preferred_element_type=jnp.float32
            )
            power = jnp.sum(banded * banded, axis=0, keepdims=True)
            power = jnp.broadcast_to(power, (8, 256))
            for turn in (128, 64, 32, 16):
                power = power + pltpu.roll(power, turn, 1)
            scale = lax.rsqrt(power[0:1] * (1.0 / SAMPLES) + 1e-06)
            term = banded * scale
            total = term if total is None else total + term
        turned = jnp.concatenate([total[:, :128].T, total[:, 128:].T], axis=0)
        out_ref[256 * n : 256 * n + 256, :] = turned.astype(jnp.bfloat16)


def spread_kernel(x_ref, out_ref):
    for o in range(64):
        block = x_ref[:, 128 * o : 128 * o + 128]
        out_ref[(o + 3) % 64, 0] = block
        out_ref[o, 1] = block
        out_ref[(o - 3) % 64, 2] = block


def toeplitz_kernel(own_ref, out_ref, src):
    line = lax.broadcasted_iota(jnp.int32, (128, 128), 0)
    lane = lax.broadcasted_iota(jnp.int32, (128, 128), 1)
    turn = (line + lane == 127).astype(jnp.bfloat16)
    src[...] = jnp.dot(own_ref[256:512, :], turn, preferred_element_type=jnp.float32)
    zero_tile = jnp.zeros((128, 128), jnp.bfloat16)

    def channel(c, carry):
        before = jnp.zeros((128, 128), jnp.float32)
        out_ref[c, 0:128, :] = zero_tile
        for e in range(17):
            if e < 16:
                wide = jnp.broadcast_to(src[pl.ds(e * 16 + c, 1), :], (128, 128))
                rolled = pltpu.roll(wide, 1, 1, stride=1, stride_axis=0)
            else:
                rolled = jnp.zeros((128, 128), jnp.float32)
            tile = jnp.where(lane <= line, rolled, before).astype(jnp.bfloat16)
            out_ref[c, 128 * e + 128 : 128 * e + 256, :] = tile
            before = rolled
        out_ref[c, 18 * 128 : 19 * 128, :] = zero_tile
        return carry

    lax.fori_loop(0, 16, channel, 0, unroll=4)


def correlate_kernel(place_ref, toe_ref, left_ref, own_ref, right_ref, out_ref, rec, lhs_0, lhs_1, res_a, res_b, done, sems):
    for i in range(PMAX * 2 * 16 * 17 // 8):
        rec[8 * i : 8 * i + 8, :] = jnp.zeros((8, 128), jnp.float32)
    for k in range(PMAX):
        place = place_ref[k]
        row = pl.multiple_of(place_ref[16 + k], 256)

        for side, ref in enumerate((left_ref, own_ref, right_ref)):

            @pl.when(place == side)
            def _():
                rows = ref[pl.ds(row, 256), :].astype(jnp.float32)
                for b in range(16):
                    for half in range(2):
                        first = ((2 * k + b % 2) * 16 + 8 * half) * 17 + 4 + b // 2
                        at = 16 * b + 8 * half
                        rec[pl.ds(first, 8, stride=17), :] = rows[at : at + 8, :]

    lag_scale = 1.0 / (NB * math.sqrt(SAMPLES))

    def fill(lhs, c):
        zeros = jnp.zeros((8, 128), jnp.float32)
        for b in range(18):
            parts = []
            for k in range(PMAX):
                parts.append(rec[pl.ds(c * 17 + ((2 * k + b % 2) * 272 + b // 2), 8), :])
            parts.append(zeros)
            for pair in range(5):
                both = jnp.concatenate(parts[2 * pair : 2 * pair + 2], axis=0).astype(jnp.bfloat16)
                lhs[16 * pair : 16 * pair + 16, 128 * b : 128 * b + 128] = both

    def work(lhs, c):
        matrix = jnp.concatenate([toe_ref[c, 128:2432, :], toe_ref[c, 0:2304, :]], axis=1)
        found = jnp.dot(lhs[...], matrix, preferred_element_type=jnp.float32)
        for k in range(PMAX):
            piece = found[8 * k : 8 * k + 8, :] * lag_scale
            res_a[pl.ds(k * 128 + c, 8, stride=16), :] = piece[:, :128]
            res_b[pl.ds(k * 128 + c, 8, stride=16), :] = piece[:, 128:]

    def four(i, carry):
        fill(lhs_0, 4 * i)
        fill(lhs_1, 4 * i + 1)
        work(lhs_0, 4 * i)
        fill(lhs_0, 4 * i + 2)
        work(lhs_1, 4 * i + 1)
        fill(lhs_1, 4 * i + 3)
        work(lhs_0, 4 * i + 2)
        work(lhs_1, 4 * i + 3)
        return carry

    copies = []
    for half in range(2):
        lax.fori_loop(2 * half, 2 * half + 2, four, 0)
        for k in range(PMAX):
            parts = []
            for m in range(8):
                at = k * 128 + 16 * m + 8 * half
                parts.append(res_a[at : at + 8, :])
                parts.append(res_b[at : at + 8, :])
            done[half, k] = jnp.concatenate(parts, axis=1)[:, SHIFT : SHIFT + LAGS]
        copies.append(pltpu.make_async_copy(done.at[half], out_ref.at[:, pl.ds(8 * half, 8), :], sems.at[half]))
        copies[half].start()
    for copy in copies:
        copy.wait()


def call(kernel, out, args, scalars=0, scratch=(), flops=0, copied_out=False):
    vmem = pl.BlockSpec(memory_space=pltpu.VMEM)
    smem = pl.BlockSpec(memory_space=pltpu.SMEM)
    size = sum(math.prod(a.shape) * a.dtype.itemsize for a in args) + math.prod(out.shape) * out.dtype.itemsize
    return pl.pallas_call(
        kernel,
        out_shape=out,
        in_specs=[smem] * scalars + [vmem] * (len(args) - scalars),
        out_specs=pl.BlockSpec(memory_space=pl.ANY) if copied_out else vmem,
        scratch_shapes=list(scratch),
        compiler_params=pltpu.CompilerParams(vmem_limit_bytes=VMEM_LIMIT),
        cost_estimate=pl.CostEstimate(flops=flops, bytes_accessed=size, transcendentals=0),
    )(*args)


def on_device(records, band_edges, receiver_block, slot_count):
    bf16 = jnp.bfloat16
    sent = call(spread_kernel, jax.ShapeDtypeStruct((64, 3, 4, 128), bf16), (records,))
    got = lax.all_to_all(sent, "tm", 0, 0, tiled=True)
    filters = call(
        filter_kernel, jax.ShapeDtypeStruct((512, 384), bf16), (taps_row(band_edges),), flops=2 * 512 * 384 * 128
    )
    shuffled = call(shuffle_kernel, jax.ShapeDtypeStruct((8, 48, 256), bf16), (got,))
    rows = lax.all_to_all(shuffled, "grp", 0, 0, tiled=True)
    own = call(
        whiten_kernel, jax.ShapeDtypeStruct((768, 128), bf16), (filters, rows), flops=2 * 3 * 512 * 384 * 256
    )
    size = lax.axis_size("tm")
    left = lax.ppermute(own, "tm", [(i, (i + 1) % size) for i in range(size)])
    right = lax.ppermute(own, "tm", [(i, (i - 1) % size) for i in range(size)])
    toe = call(
        toeplitz_kernel,
        jax.ShapeDtypeStruct((16, 2432, 128), bf16),
        (own,),
        scratch=[pltpu.VMEM((256, 128), jnp.float32)],
        flops=2 * 16 * 2432 * 128 * 256,
    )
    position = jnp.clip(receiver_block[0] - lax.axis_index("tm") + R, 0, 2 * R)
    live = jnp.arange(PMAX) < slot_count[0]
    places = jnp.concatenate(
        [
            jnp.where(live, position % 3, -1),
            jnp.zeros((16 - PMAX,), jnp.int32),
            256 * (position // 3),
            jnp.zeros((16 - PMAX,), jnp.int32),
        ]
    ).astype(jnp.int32)
    return call(
        correlate_kernel,
        jax.ShapeDtypeStruct((PMAX, 16, LAGS), jnp.float32),
        (places, toe, left, own, right),
        scalars=1,
        scratch=[
            pltpu.VMEM((PMAX * 544, 128), jnp.float32),
            pltpu.VMEM((80, 2304), bf16),
            pltpu.VMEM((80, 2304), bf16),
            pltpu.VMEM((PMAX * 128, 128), jnp.float32),
            pltpu.VMEM((PMAX * 128, 128), jnp.float32),
            pltpu.VMEM((2, PMAX, 8, LAGS), jnp.float32),
            pltpu.SemaphoreType.DMA((2,)),
        ],
        copied_out=True,
        flops=2 * 16 * 80 * 2304 * 256,
    )


def solution(mesh):
    return jax.shard_map(
        on_device,
        mesh=mesh,
        in_specs=(P(("tm", "grp"), None), P(), P("tm", None), P("tm")),
        out_specs=P("tm", "grp", None),
        check_vma=False,
    )
```

```python
import math

import jax
import jax.numpy as jnp
from jax import lax
from jax.experimental import pallas as pl
from jax.experimental.pallas import tpu as pltpu
from jax.sharding import PartitionSpec as P

TAPS = 101
NB = 4
LAG = 1000
R = 4
PMAX = 9
HALF = 50
LAGS = 2001
SAMPLES = 2048
SHIFT = 24
VMEM_LIMIT = 32 * 1024 * 1024


def taps_row(band_edges):
    tap = 178 - jnp.arange(384)
    sample_index = tap.astype(jnp.float32)
    offset = sample_index - HALF
    frequency = band_edges.astype(jnp.float32) / 256.0
    lower = frequency[:, 0:1]
    upper = frequency[:, 1:2]
    safe = jnp.where(offset == 0, 1.0, offset)
    ideal = (
        jnp.sin(2.0 * math.pi * upper * safe) - jnp.sin(2.0 * math.pi * lower * safe)
    ) / (math.pi * safe)
    ideal = jnp.where(offset == 0, 2.0 * (upper - lower), ideal)
    hamming = 0.54 - 0.46 * jnp.cos(2.0 * math.pi * sample_index / (TAPS - 1))
    taps = (ideal * hamming).astype(jnp.bfloat16)
    live = (tap >= 0) & (tap < TAPS)
    return jnp.where(live[None, :], taps, jnp.bfloat16(0)).astype(jnp.float32)


def strided(row, rows):
    wide = jnp.broadcast_to(row, (rows, row.shape[1]))
    return pltpu.roll(wide, 0, 1, stride=1, stride_axis=0)


def filter_kernel(taps_ref, out_ref):
    natural = lax.broadcasted_iota(jnp.int32, (128, 128), 0)
    order = lax.broadcasted_iota(jnp.int32, (128, 128), 1)
    time = ((order >> 2) & 3) * 32 + (order >> 4) * 4 + (order & 3)
    pick = (natural == time).astype(jnp.bfloat16)
    lane = lax.broadcasted_iota(jnp.int32, (128, 128), 1)
    row = lax.broadcasted_iota(jnp.int32, (128, 128), 0)
    for band in range(NB):
        before = None
        for part in range(3):
            piece = taps_ref[band : band + 1, part * 128 : (part + 1) * 128]
            rolled = strided(piece, 128)
            last = jnp.zeros_like(rolled) if before is None else before
            block = jnp.where(lane >= row, rolled, last).astype(jnp.bfloat16)
            ordered = jnp.dot(block, pick, preferred_element_type=jnp.float32)
            out_ref[band * 128 : (band + 1) * 128, part * 128 : (part + 1) * 128] = ordered.astype(jnp.bfloat16)
            before = rolled


def shuffle_kernel(x_ref, out_ref):
    group = lax.broadcasted_iota(jnp.int32, (16, 128), 1) >> 4
    for n in range(3):
        for tile in range(2):
            rows = []
            for b in range(8 * tile, 8 * tile + 8):
                parts = [x_ref[4 * b + q, n].astype(jnp.float32) for q in range(4)]
                rows.append(jnp.concatenate(parts, axis=0))
            for g in range(8):
                total = None
                for l in range(8):
                    turn = (16 * (l - g)) % 128
                    moved = rows[l] if turn == 0 else pltpu.roll(rows[l], turn, 1)
                    total = moved if total is None else jnp.where(group == l, moved, total)
                out_ref[g, 16 * n : 16 * n + 16, 128 * tile : 128 * tile + 128] = total.astype(jnp.bfloat16)


def whiten_kernel(filter_ref, x_ref, out_ref):
    lane = lax.broadcasted_iota(jnp.int32, (128, 256), 1)
    for n in range(3):
        here = jnp.concatenate([x_ref[g, 16 * n : 16 * n + 16, :] for g in range(8)], axis=0)
        wide = here.astype(jnp.float32)
        before = jnp.where(lane < 16, 0.0, pltpu.roll(wide, 16, 1)).astype(jnp.bfloat16)
        after = jnp.where(lane >= 240, 0.0, pltpu.roll(wide, 240, 1)).astype(jnp.bfloat16)
        window = jnp.concatenate([before, here, after], axis=0)
        total = None
        for band in range(NB):
            banded = jnp.dot(
                filter_ref[band * 128 : (band + 1) * 128, :], window, preferred_element_type=jnp.float32
            )
            power = jnp.sum(banded * banded, axis=0, keepdims=True)
            power = jnp.broadcast_to(power, (8, 256))
            for turn in (128, 64, 32, 16):
                power = power + pltpu.roll(power, turn, 1)
            scale = lax.rsqrt(power[0:1] * (1.0 / SAMPLES) + 1e-06)
            term = banded * scale
            total = term if total is None else total + term
        turned = jnp.concatenate([total[:, :128].T, total[:, 128:].T], axis=0)
        out_ref[256 * n : 256 * n + 256, :] = turned.astype(jnp.bfloat16)


def spread_kernel(x_ref, out_ref, sems):
    parts = ((0, 61, 3, 0), (61, 3, 0, 0), (0, 64, 0, 1), (3, 61, 0, 2), (0, 3, 61, 2))
    copies = []
    for i, (start, size, at, n) in enumerate(parts):
        copies.append(
            pltpu.make_async_copy(x_ref.at[pl.ds(start, size)], out_ref.at[pl.ds(at, size), n], sems.at[i])
        )
    for copy in copies:
        copy.start()
    for copy in copies:
        copy.wait()


def toeplitz_kernel(own_ref, out_ref, src):
    line = lax.broadcasted_iota(jnp.int32, (128, 128), 0)
    lane = lax.broadcasted_iota(jnp.int32, (128, 128), 1)
    turn = (line + lane == 127).astype(jnp.bfloat16)
    src[...] = jnp.dot(own_ref[256:512, :], turn, preferred_element_type=jnp.float32)
    zero_tile = jnp.zeros((128, 128), jnp.bfloat16)

    def channel(c, carry):
        before = jnp.zeros((128, 128), jnp.float32)
        out_ref[c, 0:128, :] = zero_tile
        for e in range(17):
            if e < 16:
                wide = jnp.broadcast_to(src[pl.ds(e * 16 + c, 1), :], (128, 128))
                rolled = pltpu.roll(wide, 1, 1, stride=1, stride_axis=0)
            else:
                rolled = jnp.zeros((128, 128), jnp.float32)
            tile = jnp.where(lane <= line, rolled, before).astype(jnp.bfloat16)
            out_ref[c, 128 * e + 128 : 128 * e + 256, :] = tile
            before = rolled
        out_ref[c, 18 * 128 : 19 * 128, :] = zero_tile
        return carry

    lax.fori_loop(0, 16, channel, 0, unroll=4)


def correlate_kernel(place_ref, toe_ref, left_ref, own_ref, right_ref, out_ref, rec, lhs_0, lhs_1, res_a, res_b, done, sems):
    for i in range(PMAX * 2 * 16 * 17 // 8):
        rec[8 * i : 8 * i + 8, :] = jnp.zeros((8, 128), jnp.float32)
    for k in range(PMAX):
        place = place_ref[k]
        row = pl.multiple_of(place_ref[16 + k], 256)

        for side, ref in enumerate((left_ref, own_ref, right_ref)):

            @pl.when(place == side)
            def _():
                rows = ref[pl.ds(row, 256), :].astype(jnp.float32)
                for b in range(16):
                    for half in range(2):
                        first = ((2 * k + b % 2) * 16 + 8 * half) * 17 + 4 + b // 2
                        at = 16 * b + 8 * half
                        rec[pl.ds(first, 8, stride=17), :] = rows[at : at + 8, :]

    lag_scale = 1.0 / (NB * math.sqrt(SAMPLES))

    def fill(lhs, c):
        zeros = jnp.zeros((8, 128), jnp.float32)
        for b in range(18):
            parts = []
            for k in range(PMAX):
                parts.append(rec[pl.ds(c * 17 + ((2 * k + b % 2) * 272 + b // 2), 8), :])
            parts.append(zeros)
            for pair in range(5):
                both = jnp.concatenate(parts[2 * pair : 2 * pair + 2], axis=0).astype(jnp.bfloat16)
                lhs[16 * pair : 16 * pair + 16, 128 * b : 128 * b + 128] = both

    def work(lhs, c):
        matrix = jnp.concatenate([toe_ref[c, 128:2432, :], toe_ref[c, 0:2304, :]], axis=1)
        found = jnp.dot(lhs[...], matrix, preferred_element_type=jnp.float32)
        for k in range(PMAX):
            piece = found[8 * k : 8 * k + 8, :] * lag_scale
            res_a[pl.ds(k * 128 + c, 8, stride=16), :] = piece[:, :128]
            res_b[pl.ds(k * 128 + c, 8, stride=16), :] = piece[:, 128:]

    def four(i, carry):
        fill(lhs_0, 4 * i)
        fill(lhs_1, 4 * i + 1)
        work(lhs_0, 4 * i)
        fill(lhs_0, 4 * i + 2)
        work(lhs_1, 4 * i + 1)
        fill(lhs_1, 4 * i + 3)
        work(lhs_0, 4 * i + 2)
        work(lhs_1, 4 * i + 3)
        return carry

    copies = []
    for half in range(2):
        lax.fori_loop(2 * half, 2 * half + 2, four, 0)
        for k in range(PMAX):
            parts = []
            for m in range(8):
                at = k * 128 + 16 * m + 8 * half
                parts.append(res_a[at : at + 8, :])
                parts.append(res_b[at : at + 8, :])
            done[half, k] = jnp.concatenate(parts, axis=1)[:, SHIFT : SHIFT + LAGS]
            copy = pltpu.make_async_copy(
                done.at[half, k], out_ref.at[k, pl.ds(8 * half, 8), :], sems.at[half, k]
            )
            copy.start()
            copies.append(copy)
    for copy in copies:
        copy.wait()


def call(kernel, out, args, scalars=0, scratch=(), flops=0, copied_out=False):
    vmem = pl.BlockSpec(memory_space=pltpu.VMEM)
    smem = pl.BlockSpec(memory_space=pltpu.SMEM)
    size = sum(math.prod(a.shape) * a.dtype.itemsize for a in args) + math.prod(out.shape) * out.dtype.itemsize
    return pl.pallas_call(
        kernel,
        out_shape=out,
        in_specs=[smem] * scalars + [vmem] * (len(args) - scalars),
        out_specs=pl.BlockSpec(memory_space=pl.ANY) if copied_out else vmem,
        scratch_shapes=list(scratch),
        compiler_params=pltpu.CompilerParams(vmem_limit_bytes=VMEM_LIMIT),
        cost_estimate=pl.CostEstimate(flops=flops, bytes_accessed=size, transcendentals=0),
    )(*args)


def on_device(records, band_edges, receiver_block, slot_count):
    bf16 = jnp.bfloat16
    sent = pl.pallas_call(
        spread_kernel,
        out_shape=jax.ShapeDtypeStruct((64, 3, 4, 128), bf16),
        in_specs=[pl.BlockSpec(memory_space=pltpu.HBM)],
        out_specs=pl.BlockSpec(memory_space=pl.ANY),
        scratch_shapes=[pltpu.SemaphoreType.DMA((5,))],
        compiler_params=pltpu.CompilerParams(vmem_limit_bytes=62 * 1024 * 1024),
    )(records.reshape(4, 64, 128).transpose(1, 0, 2))
    got = lax.all_to_all(sent, "tm", 0, 0, tiled=True)
    filters = call(
        filter_kernel, jax.ShapeDtypeStruct((512, 384), bf16), (taps_row(band_edges),), flops=2 * 512 * 384 * 128
    )
    shuffled = call(shuffle_kernel, jax.ShapeDtypeStruct((8, 48, 256), bf16), (got,))
    rows = lax.all_to_all(shuffled, "grp", 0, 0, tiled=True)
    own = call(
        whiten_kernel, jax.ShapeDtypeStruct((768, 128), bf16), (filters, rows), flops=2 * 3 * 512 * 384 * 256
    )
    size = lax.axis_size("tm")
    left = lax.ppermute(own, "tm", [(i, (i + 1) % size) for i in range(size)])
    right = lax.ppermute(own, "tm", [(i, (i - 1) % size) for i in range(size)])
    toe = call(
        toeplitz_kernel,
        jax.ShapeDtypeStruct((16, 2432, 128), bf16),
        (own,),
        scratch=[pltpu.VMEM((256, 128), jnp.float32)],
        flops=2 * 16 * 2432 * 128 * 256,
    )
    position = jnp.clip(receiver_block[0] - lax.axis_index("tm") + R, 0, 2 * R)
    live = jnp.arange(PMAX) < slot_count[0]
    places = jnp.concatenate(
        [
            jnp.where(live, position % 3, -1),
            jnp.zeros((16 - PMAX,), jnp.int32),
            256 * (position // 3),
            jnp.zeros((16 - PMAX,), jnp.int32),
        ]
    ).astype(jnp.int32)
    return call(
        correlate_kernel,
        jax.ShapeDtypeStruct((PMAX, 16, LAGS), jnp.float32),
        (places, toe, left, own, right),
        scalars=1,
        scratch=[
            pltpu.VMEM((PMAX * 544, 128), jnp.float32),
            pltpu.VMEM((80, 2304), bf16),
            pltpu.VMEM((80, 2304), bf16),
            pltpu.VMEM((PMAX * 128, 128), jnp.float32),
            pltpu.VMEM((PMAX * 128, 128), jnp.float32),
            pltpu.VMEM((2, PMAX, 8, LAGS), jnp.float32),
            pltpu.SemaphoreType.DMA((2, PMAX)),
        ],
        copied_out=True,
        flops=2 * 16 * 80 * 2304 * 256,
    )


def solution(mesh):
    return jax.shard_map(
        on_device,
        mesh=mesh,
        in_specs=(P(("tm", "grp"), None), P(), P("tm", None), P("tm")),
        out_specs=P("tm", "grp", None),
        check_vma=False,
    )
```

```python
import math

import jax
import jax.numpy as jnp
from jax import lax
from jax.experimental import pallas as pl
from jax.experimental.pallas import tpu as pltpu
from jax.sharding import PartitionSpec as P

TAPS = 101
NB = 4
LAG = 1000
R = 4
PMAX = 9
HALF = 50
LAGS = 2001
SAMPLES = 2048
SHIFT = 24
VMEM_LIMIT = 32 * 1024 * 1024


def taps_row(band_edges):
    tap = 178 - jnp.arange(384)
    sample_index = tap.astype(jnp.float32)
    offset = sample_index - HALF
    frequency = band_edges.astype(jnp.float32) / 256.0
    lower = frequency[:, 0:1]
    upper = frequency[:, 1:2]
    safe = jnp.where(offset == 0, 1.0, offset)
    ideal = (
        jnp.sin(2.0 * math.pi * upper * safe) - jnp.sin(2.0 * math.pi * lower * safe)
    ) / (math.pi * safe)
    ideal = jnp.where(offset == 0, 2.0 * (upper - lower), ideal)
    hamming = 0.54 - 0.46 * jnp.cos(2.0 * math.pi * sample_index / (TAPS - 1))
    taps = (ideal * hamming).astype(jnp.bfloat16)
    live = (tap >= 0) & (tap < TAPS)
    return jnp.where(live[None, :], taps, jnp.bfloat16(0)).astype(jnp.float32)


def strided(row, rows):
    wide = jnp.broadcast_to(row, (rows, row.shape[1]))
    return pltpu.roll(wide, 0, 1, stride=1, stride_axis=0)


def filter_kernel(taps_ref, out_ref):
    natural = lax.broadcasted_iota(jnp.int32, (128, 128), 0)
    order = lax.broadcasted_iota(jnp.int32, (128, 128), 1)
    time = ((order >> 2) & 3) * 32 + (order >> 4) * 4 + (order & 3)
    pick = (natural == time).astype(jnp.bfloat16)
    lane = lax.broadcasted_iota(jnp.int32, (128, 128), 1)
    row = lax.broadcasted_iota(jnp.int32, (128, 128), 0)
    for band in range(NB):
        before = None
        for part in range(3):
            piece = taps_ref[band : band + 1, part * 128 : (part + 1) * 128]
            rolled = strided(piece, 128)
            last = jnp.zeros_like(rolled) if before is None else before
            block = jnp.where(lane >= row, rolled, last).astype(jnp.bfloat16)
            ordered = jnp.dot(block, pick, preferred_element_type=jnp.float32)
            out_ref[band * 128 : (band + 1) * 128, part * 128 : (part + 1) * 128] = ordered.astype(jnp.bfloat16)
            before = rolled


def shuffle_kernel(x_ref, out_ref):
    group = lax.broadcasted_iota(jnp.int32, (16, 128), 1) >> 4
    for n in range(3):
        for tile in range(2):
            rows = []
            for b in range(8 * tile, 8 * tile + 8):
                parts = [x_ref[4 * b + q, n].astype(jnp.float32) for q in range(4)]
                rows.append(jnp.concatenate(parts, axis=0))
            for step in (4, 2, 1):
                upper = (group & step) != 0
                for i in range(8):
                    if i & step:
                        continue
                    low, high = rows[i], rows[i + step]
                    rows[i] = jnp.where(upper, pltpu.roll(high, 16 * step, 1), low)
                    rows[i + step] = jnp.where(upper, high, pltpu.roll(low, 128 - 16 * step, 1))
            for g in range(8):
                out_ref[g, 16 * n : 16 * n + 16, 128 * tile : 128 * tile + 128] = rows[g].astype(jnp.bfloat16)


def whiten_kernel(filter_ref, x_ref, out_ref):
    lane = lax.broadcasted_iota(jnp.int32, (128, 256), 1)
    for n in range(3):
        here = jnp.concatenate([x_ref[g, 16 * n : 16 * n + 16, :] for g in range(8)], axis=0)
        wide = here.astype(jnp.float32)
        before = jnp.where(lane < 16, 0.0, pltpu.roll(wide, 16, 1)).astype(jnp.bfloat16)
        after = jnp.where(lane >= 240, 0.0, pltpu.roll(wide, 240, 1)).astype(jnp.bfloat16)
        window = jnp.concatenate([before, here, after], axis=0)
        total = None
        for band in range(NB):
            banded = jnp.dot(
                filter_ref[band * 128 : (band + 1) * 128, :], window, preferred_element_type=jnp.float32
            )
            power = jnp.sum(banded * banded, axis=0, keepdims=True)
            power = jnp.broadcast_to(power, (8, 256))
            for turn in (128, 64, 32, 16):
                power = power + pltpu.roll(power, turn, 1)
            scale = lax.rsqrt(power[0:1] * (1.0 / SAMPLES) + 1e-06)
            term = banded * scale
            total = term if total is None else total + term
        turned = jnp.concatenate([total[:, :128].T, total[:, 128:].T], axis=0)
        out_ref[256 * n : 256 * n + 256, :] = turned.astype(jnp.bfloat16)


def spread_kernel(x_ref, out_ref):
    for o in range(64):
        block = x_ref[:, 128 * o : 128 * o + 128]
        out_ref[(o + 3) % 64, 0] = block
        out_ref[o, 1] = block
        out_ref[(o - 3) % 64, 2] = block


def toeplitz_kernel(own_ref, out_ref, src):
    line = lax.broadcasted_iota(jnp.int32, (128, 128), 0)
    lane = lax.broadcasted_iota(jnp.int32, (128, 128), 1)
    turn = (line + lane == 127).astype(jnp.bfloat16)
    src[...] = jnp.dot(own_ref[256:512, :], turn, preferred_element_type=jnp.float32)
    zero_tile = jnp.zeros((128, 128), jnp.bfloat16)

    def channel(c, carry):
        before = jnp.zeros((128, 128), jnp.float32)
        out_ref[c, 0:128, :] = zero_tile
        for e in range(17):
            if e < 16:
                wide = jnp.broadcast_to(src[pl.ds(e * 16 + c, 1), :], (128, 128))
                rolled = pltpu.roll(wide, 1, 1, stride=1, stride_axis=0)
            else:
                rolled = jnp.zeros((128, 128), jnp.float32)
            tile = jnp.where(lane <= line, rolled, before).astype(jnp.bfloat16)
            out_ref[c, 128 * e + 128 : 128 * e + 256, :] = tile
            before = rolled
        out_ref[c, 18 * 128 : 19 * 128, :] = zero_tile
        return carry

    lax.fori_loop(0, 16, channel, 0, unroll=4)


def correlate_kernel(place_ref, toe_ref, left_ref, own_ref, right_ref, out_ref, rec, lhs, res_a, res_b, done, sems):
    for i in range(PMAX * 2 * 16 * 17 // 8):
        rec[8 * i : 8 * i + 8, :] = jnp.zeros((8, 128), jnp.float32)
    for k in range(PMAX):
        place = place_ref[k]
        row = pl.multiple_of(place_ref[16 + k], 256)

        for side, ref in enumerate((left_ref, own_ref, right_ref)):

            @pl.when(place == side)
            def _():
                rows = ref[pl.ds(row, 256), :].astype(jnp.float32)
                for b in range(16):
                    for half in range(2):
                        first = ((2 * k + b % 2) * 16 + 8 * half) * 17 + 4 + b // 2
                        at = 16 * b + 8 * half
                        rec[pl.ds(first, 8, stride=17), :] = rows[at : at + 8, :]

    lag_scale = 1.0 / (NB * math.sqrt(SAMPLES))

    def fill(lhs, c):
        zeros = jnp.zeros((8, 128), jnp.float32)
        for b in range(18):
            parts = []
            for k in range(PMAX):
                parts.append(rec[pl.ds(c * 17 + ((2 * k + b % 2) * 272 + b // 2), 8), :])
            parts.append(zeros)
            for pair in range(5):
                both = jnp.concatenate(parts[2 * pair : 2 * pair + 2], axis=0).astype(jnp.bfloat16)
                lhs[16 * pair : 16 * pair + 16, 128 * b : 128 * b + 128] = both

    def work(lhs, c):
        matrix = jnp.concatenate([toe_ref[c, 128:2432, :], toe_ref[c, 0:2304, :]], axis=1)
        found = jnp.dot(lhs[...], matrix, preferred_element_type=jnp.float32)
        for k in range(PMAX):
            piece = found[8 * k : 8 * k + 8, :] * lag_scale
            res_a[pl.ds(k * 128 + c, 8, stride=16), :] = piece[:, :128]
            res_b[pl.ds(k * 128 + c, 8, stride=16), :] = piece[:, 128:]

    copies = []
    for half in range(2):
        for c in range(8 * half, 8 * half + 8):
            fill(lhs.at[c % 4], c)
            if c % 8 >= 1:
                work(lhs.at[(c - 1) % 4], c - 1)
        work(lhs.at[3], 8 * half + 7)
        for k in range(PMAX):
            parts = []
            for m in range(8):
                at = k * 128 + 16 * m + 8 * half
                parts.append(res_a[at : at + 8, :])
                parts.append(res_b[at : at + 8, :])
            done[half, k] = jnp.concatenate(parts, axis=1)[:, SHIFT : SHIFT + LAGS]
            copy = pltpu.make_async_copy(
                done.at[half, k], out_ref.at[k, pl.ds(8 * half, 8), :], sems.at[half, k]
            )
            copy.start()
            copies.append(copy)
    for copy in copies:
        copy.wait()


def call(kernel, out, args, scalars=0, scratch=(), flops=0, copied_out=False):
    vmem = pl.BlockSpec(memory_space=pltpu.VMEM)
    smem = pl.BlockSpec(memory_space=pltpu.SMEM)
    size = sum(math.prod(a.shape) * a.dtype.itemsize for a in args) + math.prod(out.shape) * out.dtype.itemsize
    return pl.pallas_call(
        kernel,
        out_shape=out,
        in_specs=[smem] * scalars + [vmem] * (len(args) - scalars),
        out_specs=pl.BlockSpec(memory_space=pl.ANY) if copied_out else vmem,
        scratch_shapes=list(scratch),
        compiler_params=pltpu.CompilerParams(vmem_limit_bytes=VMEM_LIMIT),
        cost_estimate=pl.CostEstimate(flops=flops, bytes_accessed=size, transcendentals=0),
    )(*args)


def on_device(records, band_edges, receiver_block, slot_count):
    bf16 = jnp.bfloat16
    sent = call(spread_kernel, jax.ShapeDtypeStruct((64, 3, 4, 128), bf16), (records,))
    got = lax.all_to_all(sent, "tm", 0, 0, tiled=True)
    filters = call(
        filter_kernel, jax.ShapeDtypeStruct((512, 384), bf16), (taps_row(band_edges),), flops=2 * 512 * 384 * 128
    )
    shuffled = call(shuffle_kernel, jax.ShapeDtypeStruct((8, 48, 256), bf16), (got,))
    rows = lax.all_to_all(shuffled, "grp", 0, 0, tiled=True)
    own = call(
        whiten_kernel, jax.ShapeDtypeStruct((768, 128), bf16), (filters, rows), flops=2 * 3 * 512 * 384 * 256
    )
    size = lax.axis_size("tm")
    left = lax.ppermute(own, "tm", [(i, (i + 1) % size) for i in range(size)])
    right = lax.ppermute(own, "tm", [(i, (i - 1) % size) for i in range(size)])
    toe = call(
        toeplitz_kernel,
        jax.ShapeDtypeStruct((16, 2432, 128), bf16),
        (own,),
        scratch=[pltpu.VMEM((256, 128), jnp.float32)],
        flops=2 * 16 * 2432 * 128 * 256,
    )
    position = jnp.clip(receiver_block[0] - lax.axis_index("tm") + R, 0, 2 * R)
    live = jnp.arange(PMAX) < slot_count[0]
    places = jnp.concatenate(
        [
            jnp.where(live, position % 3, -1),
            jnp.zeros((16 - PMAX,), jnp.int32),
            256 * (position // 3),
            jnp.zeros((16 - PMAX,), jnp.int32),
        ]
    ).astype(jnp.int32)
    return call(
        correlate_kernel,
        jax.ShapeDtypeStruct((PMAX, 16, LAGS), jnp.float32),
        (places, toe, left, own, right),
        scalars=1,
        scratch=[
            pltpu.VMEM((PMAX * 544, 128), jnp.float32),
            pltpu.VMEM((4, 80, 2304), bf16),
            pltpu.VMEM((PMAX * 128, 128), jnp.float32),
            pltpu.VMEM((PMAX * 128, 128), jnp.float32),
            pltpu.VMEM((2, PMAX, 8, LAGS), jnp.float32),
            pltpu.SemaphoreType.DMA((2, PMAX)),
        ],
        copied_out=True,
        flops=2 * 16 * 80 * 2304 * 256,
    )


def solution(mesh):
    return jax.shard_map(
        on_device,
        mesh=mesh,
        in_specs=(P(("tm", "grp"), None), P(), P("tm", None), P("tm")),
        out_specs=P("tm", "grp", None),
        check_vma=False,
    )
```

```python
import math

import jax
import jax.numpy as jnp
from jax import lax
from jax.experimental import pallas as pl
from jax.experimental.pallas import tpu as pltpu
from jax.sharding import PartitionSpec as P

TAPS = 101
NB = 4
LAG = 1000
R = 4
PMAX = 9
HALF = 50
LAGS = 2001
SAMPLES = 2048
SHIFT = 24
VMEM_LIMIT = 32 * 1024 * 1024


def taps_row(band_edges):
    tap = 178 - jnp.arange(384)
    sample_index = tap.astype(jnp.float32)
    offset = sample_index - HALF
    frequency = band_edges.astype(jnp.float32) / 256.0
    lower = frequency[:, 0:1]
    upper = frequency[:, 1:2]
    safe = jnp.where(offset == 0, 1.0, offset)
    ideal = (
        jnp.sin(2.0 * math.pi * upper * safe) - jnp.sin(2.0 * math.pi * lower * safe)
    ) / (math.pi * safe)
    ideal = jnp.where(offset == 0, 2.0 * (upper - lower), ideal)
    hamming = 0.54 - 0.46 * jnp.cos(2.0 * math.pi * sample_index / (TAPS - 1))
    taps = (ideal * hamming).astype(jnp.bfloat16)
    live = (tap >= 0) & (tap < TAPS)
    return jnp.where(live[None, :], taps, jnp.bfloat16(0)).astype(jnp.float32)


def strided(row, rows):
    wide = jnp.broadcast_to(row, (rows, row.shape[1]))
    return pltpu.roll(wide, 0, 1, stride=1, stride_axis=0)


def filter_kernel(taps_ref, out_ref):
    natural = lax.broadcasted_iota(jnp.int32, (128, 128), 0)
    order = lax.broadcasted_iota(jnp.int32, (128, 128), 1)
    time = ((order >> 2) & 3) * 32 + (order >> 4) * 4 + (order & 3)
    pick = (natural == time).astype(jnp.bfloat16)
    lane = lax.broadcasted_iota(jnp.int32, (128, 128), 1)
    row = lax.broadcasted_iota(jnp.int32, (128, 128), 0)
    for band in range(NB):
        before = None
        for part in range(3):
            piece = taps_ref[band : band + 1, part * 128 : (part + 1) * 128]
            rolled = strided(piece, 128)
            last = jnp.zeros_like(rolled) if before is None else before
            block = jnp.where(lane >= row, rolled, last).astype(jnp.bfloat16)
            ordered = jnp.dot(block, pick, preferred_element_type=jnp.float32)
            out_ref[band * 128 : (band + 1) * 128, part * 128 : (part + 1) * 128] = ordered.astype(jnp.bfloat16)
            before = rolled


def shuffle_kernel(x_ref, out_ref):
    group = lax.broadcasted_iota(jnp.int32, (16, 128), 1) >> 4
    for n in range(3):
        for tile in range(2):
            rows = []
            for b in range(8 * tile, 8 * tile + 8):
                parts = [x_ref[4 * b + q, n].astype(jnp.float32) for q in range(4)]
                rows.append(jnp.concatenate(parts, axis=0))
            for step in (4, 2, 1):
                upper = (group & step) != 0
                for i in range(8):
                    if i & step:
                        continue
                    low, high = rows[i], rows[i + step]
                    rows[i] = jnp.where(upper, pltpu.roll(high, 16 * step, 1), low)
                    rows[i + step] = jnp.where(upper, high, pltpu.roll(low, 128 - 16 * step, 1))
            for g in range(8):
                out_ref[g, 16 * n : 16 * n + 16, 128 * tile : 128 * tile + 128] = rows[g].astype(jnp.bfloat16)


def whiten_kernel(filter_ref, x_ref, out_ref):
    lane = lax.broadcasted_iota(jnp.int32, (128, 256), 1)
    for n in range(3):
        here = jnp.concatenate([x_ref[g, 16 * n : 16 * n + 16, :] for g in range(8)], axis=0)
        wide = here.astype(jnp.float32)
        before = jnp.where(lane < 16, 0.0, pltpu.roll(wide, 16, 1)).astype(jnp.bfloat16)
        after = jnp.where(lane >= 240, 0.0, pltpu.roll(wide, 240, 1)).astype(jnp.bfloat16)
        window = jnp.concatenate([before, here, after], axis=0)
        total = None
        for band in range(NB):
            banded = jnp.dot(
                filter_ref[band * 128 : (band + 1) * 128, :], window, preferred_element_type=jnp.float32
            )
            power = jnp.sum(banded * banded, axis=0, keepdims=True)
            power = jnp.broadcast_to(power, (8, 256))
            for turn in (128, 64, 32, 16):
                power = power + pltpu.roll(power, turn, 1)
            scale = lax.rsqrt(power[0:1] * (1.0 / SAMPLES) + 1e-06)
            term = banded * scale
            total = term if total is None else total + term
        turned = jnp.concatenate([total[:, :128].T, total[:, 128:].T], axis=0)
        out_ref[256 * n : 256 * n + 256, :] = turned.astype(jnp.bfloat16)


def spread_kernel(x_ref, out_ref):
    for o in range(64):
        block = x_ref[:, 128 * o : 128 * o + 128]
        out_ref[(o + 3) % 64, 0] = block
        out_ref[o, 1] = block
        out_ref[(o - 3) % 64, 2] = block


def toeplitz_kernel(own_ref, out_ref, src):
    line = lax.broadcasted_iota(jnp.int32, (128, 128), 0)
    lane = lax.broadcasted_iota(jnp.int32, (128, 128), 1)
    turn = (line + lane == 127).astype(jnp.bfloat16)
    src[...] = jnp.dot(own_ref[256:512, :], turn, preferred_element_type=jnp.float32)
    zero_tile = jnp.zeros((128, 128), jnp.bfloat16)

    def channel(c, carry):
        before = jnp.zeros((128, 128), jnp.float32)
        out_ref[c, 0:128, :] = zero_tile
        for e in range(17):
            if e < 16:
                wide = jnp.broadcast_to(src[pl.ds(e * 16 + c, 1), :], (128, 128))
                rolled = pltpu.roll(wide, 1, 1, stride=1, stride_axis=0)
            else:
                rolled = jnp.zeros((128, 128), jnp.float32)
            tile = jnp.where(lane <= line, rolled, before).astype(jnp.bfloat16)
            out_ref[c, 128 * e + 128 : 128 * e + 256, :] = tile
            before = rolled
        out_ref[c, 18 * 128 : 19 * 128, :] = zero_tile
        return carry

    lax.fori_loop(0, 16, channel, 0, unroll=4)


def correlate_kernel(place_ref, toe_ref, left_ref, own_ref, right_ref, out_ref, rec, lhs, res_a, res_b, done, sems):
    for i in range(PMAX * 2 * 16 * 17 // 8):
        rec[8 * i : 8 * i + 8, :] = jnp.zeros((8, 128), jnp.float32)
    for k in range(PMAX):
        place = place_ref[k]
        row = pl.multiple_of(place_ref[16 + k], 256)

        for side, ref in enumerate((left_ref, own_ref, right_ref)):

            @pl.when(place == side)
            def _():
                rows = ref[pl.ds(row, 256), :].astype(jnp.float32)
                for b in range(16):
                    for half in range(2):
                        first = ((2 * k + b % 2) * 16 + 8 * half) * 17 + 4 + b // 2
                        at = 16 * b + 8 * half
                        rec[pl.ds(first, 8, stride=17), :] = rows[at : at + 8, :]

    lag_scale = 1.0 / (NB * math.sqrt(SAMPLES))

    def fill(lhs, c):
        zeros = jnp.zeros((8, 128), jnp.float32)
        for b in range(18):
            parts = []
            for k in range(PMAX):
                parts.append(rec[pl.ds(c * 17 + ((2 * k + b % 2) * 272 + b // 2), 8), :])
            parts.append(zeros)
            for pair in range(5):
                both = jnp.concatenate(parts[2 * pair : 2 * pair + 2], axis=0).astype(jnp.bfloat16)
                lhs[16 * pair : 16 * pair + 16, 128 * b : 128 * b + 128] = both

    def work(lhs, c):
        matrix = jnp.concatenate([toe_ref[c, 128:2432, :], toe_ref[c, 0:2304, :]], axis=1)
        found = jnp.dot(lhs[...], matrix, preferred_element_type=jnp.float32)
        for k in range(PMAX):
            piece = found[8 * k : 8 * k + 8, :] * lag_scale
            res_a[pl.ds(k * 128 + c, 8, stride=16), :] = piece[:, :128]
            res_b[pl.ds(k * 128 + c, 8, stride=16), :] = piece[:, 128:]

    copies = []
    for half in range(2):
        for c in range(8 * half, 8 * half + 8):
            fill(lhs.at[c % 4], c)
            if c % 8 >= 1:
                work(lhs.at[(c - 1) % 4], c - 1)
        work(lhs.at[3], 8 * half + 7)
        for k in range(PMAX):
            parts = []
            for m in range(8):
                at = k * 128 + 16 * m + 8 * half
                parts.append(res_a[at : at + 8, :])
                parts.append(res_b[at : at + 8, :])
            done[half, k] = jnp.concatenate(parts, axis=1)[:, SHIFT : SHIFT + LAGS]
            copy = pltpu.make_async_copy(
                done.at[half, k], out_ref.at[k, pl.ds(8 * half, 8), :], sems.at[half, k]
            )
            copy.start()
            copies.append(copy)
    for copy in copies:
        copy.wait()


def call(kernel, out, args, scalars=0, scratch=(), flops=0, copied_out=False):
    vmem = pl.BlockSpec(memory_space=pltpu.VMEM)
    smem = pl.BlockSpec(memory_space=pltpu.SMEM)
    size = sum(math.prod(a.shape) * a.dtype.itemsize for a in args) + math.prod(out.shape) * out.dtype.itemsize
    return pl.pallas_call(
        kernel,
        out_shape=out,
        in_specs=[smem] * scalars + [vmem] * (len(args) - scalars),
        out_specs=pl.BlockSpec(memory_space=pl.ANY) if copied_out else vmem,
        scratch_shapes=list(scratch),
        compiler_params=pltpu.CompilerParams(vmem_limit_bytes=VMEM_LIMIT),
        cost_estimate=pl.CostEstimate(flops=flops, bytes_accessed=size, transcendentals=0),
    )(*args)


def on_device(records, band_edges, receiver_block, slot_count):
    bf16 = jnp.bfloat16
    sent = call(spread_kernel, jax.ShapeDtypeStruct((64, 3, 4, 128), bf16), (records,))
    got = lax.all_to_all(sent, "tm", 0, 0, tiled=True)
    filters = call(
        filter_kernel, jax.ShapeDtypeStruct((512, 384), bf16), (taps_row(band_edges),), flops=2 * 512 * 384 * 128
    )
    shuffled = call(shuffle_kernel, jax.ShapeDtypeStruct((8, 48, 256), bf16), (got,))
    rows = lax.all_to_all(shuffled, "grp", 0, 0, tiled=True)
    own = call(
        whiten_kernel, jax.ShapeDtypeStruct((768, 128), bf16), (filters, rows), flops=2 * 3 * 512 * 384 * 256
    )
    size = lax.axis_size("tm")
    right = lax.ppermute(own, "tm", [(i, (i - 1) % size) for i in range(size)])
    left = lax.ppermute(own, "tm", [(i, (i + 1) % size) for i in range(size)])
    toe = call(
        toeplitz_kernel,
        jax.ShapeDtypeStruct((16, 2432, 128), bf16),
        (own,),
        scratch=[pltpu.VMEM((256, 128), jnp.float32)],
        flops=2 * 16 * 2432 * 128 * 256,
    )
    position = jnp.clip(receiver_block[0] - lax.axis_index("tm") + R, 0, 2 * R)
    live = jnp.arange(PMAX) < slot_count[0]
    places = jnp.concatenate(
        [
            jnp.where(live, position % 3, -1),
            jnp.zeros((16 - PMAX,), jnp.int32),
            256 * (position // 3),
            jnp.zeros((16 - PMAX,), jnp.int32),
        ]
    ).astype(jnp.int32)
    return call(
        correlate_kernel,
        jax.ShapeDtypeStruct((PMAX, 16, LAGS), jnp.float32),
        (places, toe, left, own, right),
        scalars=1,
        scratch=[
            pltpu.VMEM((PMAX * 544, 128), jnp.float32),
            pltpu.VMEM((4, 80, 2304), bf16),
            pltpu.VMEM((PMAX * 128, 128), jnp.float32),
            pltpu.VMEM((PMAX * 128, 128), jnp.float32),
            pltpu.VMEM((2, PMAX, 8, LAGS), jnp.float32),
            pltpu.SemaphoreType.DMA((2, PMAX)),
        ],
        copied_out=True,
        flops=2 * 16 * 80 * 2304 * 256,
    )


def solution(mesh):
    return jax.shard_map(
        on_device,
        mesh=mesh,
        in_specs=(P(("tm", "grp"), None), P(), P("tm", None), P("tm")),
        out_specs=P("tm", "grp", None),
        check_vma=False,
    )
```
